32 devices in a mesh: dp: 4 (over y, x), pipe: 4 (over z), tensor: 2 (over core).
Axes of the slice: x: 2, y: 2, z: 4, core: 2. Of those that a mesh axis runs over, the one named last changes fastest.
Arguments:
- hidden: bfloat16 [4, 256, 14336], P('pipe', 'dp', 'tensor'), parts along dimension 1, may hold values from -6 to 6
- residual: bfloat16 [4, 256, 4096], P('pipe', ('dp', 'tensor')), parts along dimension 1, may hold values from -6 to 6
- norm_gain: float32 [4, 4096], P('pipe'), may hold values from 0.5 to 1.5
- down_weight: bfloat16 [4, 14336, 4096], P('pipe', 'tensor'), may hold values from -0.046875 to 0.046875
- qkv_weight: bfloat16 [4, 4096, 6144], P('pipe', None, 'tensor'), may hold values from -0.09375 to 0.09375
Outputs:
- section_output: bfloat16 [4, 256, 4096], P('pipe', ('dp', 'tensor')), parts along dimension 1
- projections: bfloat16 [4, 256, 6144], P('pipe', 'dp', 'tensor'), parts along dimension 1
The draws below stay inside these ranges and needn't reach their ends.
There are 4 independent parts, one for each index of `dp`. The reference program is written for one: setup_inputs(seed, part) draws one part's arguments, and reference() takes and returns one part's arrays. A program takes and returns all parts, laid end to end along the dimension named above; an argument that names none is the same for every part. Nothing has to cross between parts.
All inputs are finite; a program needn't handle non-finite values.
Results may differ from the reference program's by a relative error of at most 0.022.
Values may be sent and summed in bfloat16 or wider, within the bound.
A program may use at most 128 MiB of HBM per device.

```python
import jax
import jax.numpy as jnp
from jax import lax

D = 4096
FF = 14336
TOKENS = 64
QKV = 6144
SECTIONS = 4
N_TENSOR = 2


def block_levels(stream_key, extent, pieces, smallest, high):
    level = 1.0
    for position, shards_of in pieces:
        heights = jax.random.uniform(jax.random.fold_in(jax.random.fold_in(stream_key, 6), position), (shards_of,), jnp.float32, smallest / len(pieces), high / len(pieces))
        level = level * jnp.repeat(jnp.exp(heights), extent[position] // shards_of).reshape((-1,) + (1,) * (len(extent) - 1 - position))
    return level


def normal_values(rng, shape, width, limit, shards=(), kind=jnp.bfloat16):
    factor_of = block_levels(rng, shape, shards, -0.22, 0.18) if shards else 1.0
    entries = jax.random.normal(rng, shape, jnp.float32) * width * factor_of
    return jnp.minimum(jnp.maximum(entries, -limit), limit).astype(kind)


def setup_inputs(seed: int = 0, part: int = 0) -> dict:
    key_of = jax.random.split(jax.random.key(seed), 6)
    part_splits = jax.random.split(jax.random.fold_in(key_of[5], part), 6)
    return {
        "hidden": normal_values(part_splits[0], (SECTIONS, TOKENS, FF), 1.0, 6.0, ((0, 4), (2, 2))),
        "residual": normal_values(part_splits[1], (SECTIONS, TOKENS, D), 1.0, 6.0, ((0, 4), (1, 2))),
        "norm_gain": jnp.clip(1.0 + 0.1 * jax.random.normal(key_of[2], (SECTIONS, D), jnp.float32), 0.5, 1.5),
        "down_weight": normal_values(key_of[3], (SECTIONS, FF, D), FF ** -0.5, 0.046875, ((0, 4), (1, 2))),
        "qkv_weight": normal_values(key_of[4], (SECTIONS, D, QKV), D ** -0.5, 0.09375, ((0, 4), (2, 2))),
    }


def normalize(values, gain_row):
    wide = values.astype(jnp.float32)
    scaler = lax.rsqrt(lax.optimization_barrier(jnp.mean(wide * wide, axis=-1, keepdims=True)) + 1e-05)
    return (wide * scaler * gain_row.astype(jnp.float32)).astype(jnp.bfloat16)

def reference(hidden, residual, norm_gain, down_weight, qkv_weight):
    group_width = FF // N_TENSOR
    outputs = []
    for section_idx in range(SECTIONS):
        hidden_rows = hidden[section_idx]
        down_local = down_weight[section_idx]

        def add_group(running, group_idx):
            offset = (group_idx * group_width).astype(jnp.int32)
            group_term = jnp.dot(lax.dynamic_slice_in_dim(hidden_rows, offset, group_width, 1), lax.dynamic_slice_in_dim(down_local, offset, group_width, 0), preferred_element_type=jnp.float32)
            group_term = lax.optimization_barrier(group_term.astype(jnp.bfloat16)).astype(jnp.float32)
            return (running + group_term, None)
        running, _ = lax.scan(add_group, jnp.zeros((TOKENS, D), jnp.float32), jnp.arange(N_TENSOR, dtype=jnp.int32))
        outputs.append((residual[section_idx].astype(jnp.float32) + running).astype(jnp.bfloat16))
    section_output = jnp.stack(outputs)
    projected = []
    for section_idx in range(SECTIONS):
        normed = normalize(section_output[(section_idx - 1) % SECTIONS], norm_gain[section_idx])
        projected.append(jnp.dot(normed, qkv_weight[section_idx], preferred_element_type=jnp.float32).astype(jnp.bfloat16))
    return (section_output, jnp.stack(projected))
```

```python
import functools

import jax
import jax.numpy as jnp
from jax import lax
from jax.experimental import pallas as pl
from jax.experimental.pallas import tpu as pltpu
from jax.sharding import PartitionSpec as P

EPS = 1e-05
COLS = 512
K_BLOCKS = 4
MESH = pl.DeviceIdType.MESH


def passed_along(value, axis, steps):
    count = lax.axis_size(axis)
    pairs = [(source, (source + steps) % count) for source in range(count)]
    return lax.ppermute(value, axis, pairs)


def normalize(values, gain_row):
    wide = values.astype(jnp.float32)
    scaler = lax.rsqrt(jnp.mean(wide * wide, axis=-1, keepdims=True) + EPS)
    return (wide * scaler * gain_row).astype(jnp.bfloat16)


def plain_shards(hidden, residual, norm_gain, down_weight, qkv_weight):
    hidden_rows = hidden[0]
    resid_rows = residual[0]
    gain_row = norm_gain[0]
    down_local = down_weight[0]
    qkv_local = qkv_weight[0]
    tok_rows = resid_rows.shape[0]
    resid_full = lax.all_gather(resid_rows, "tensor", axis=0, tiled=True)
    summed = lax.psum(
        jnp.dot(hidden_rows, down_local, preferred_element_type=jnp.float32).astype(jnp.bfloat16),
        "tensor",
    ).astype(jnp.float32)
    full_rows = (resid_full.astype(jnp.float32) + summed).astype(jnp.bfloat16)
    offset = lax.axis_index("tensor") * tok_rows
    section_output = lax.dynamic_slice_in_dim(full_rows, offset, tok_rows, 0)
    arrived = passed_along(full_rows, "pipe", 1)
    normed = normalize(arrived, gain_row)
    projections = jnp.dot(normed, qkv_local, preferred_element_type=jnp.float32).astype(
        jnp.bfloat16
    )
    return (section_output[None], projections[None])


def boundary_kernel(
    pipes,
    hid_hbm, res_hbm, gain_hbm, down_hbm, qkv_hbm,
    out_hbm, proj_hbm,
    hid_v, res_v, gain_v, dbuf, qbuf, group, group_in, stage, x_in, out_v, proj_v, acc_v, sumsq,
    small_sem, d_sem, q_sem, o_sem, g_send, g_recv, x_send, x_recv,
):
    dp = lax.axis_index("dp")
    pipe = lax.axis_index("pipe")
    core = lax.axis_index("tensor")
    other = 1 - core
    after = lax.rem(pipe + 1, pipes)
    before = lax.rem(pipe + pipes - 1, pipes)

    tokens, units = hid_v.shape
    mine, width = res_v.shape
    chunks = width // COLS
    depth = units // K_BLOCKS
    q_cols = qbuf.shape[2]
    q_parts = q_cols // COLS
    my_rows = pl.ds(pl.multiple_of(core * mine, mine), mine)
    other_rows = pl.ds(pl.multiple_of(other * mine, mine), mine)

    def cols(c):
        return pl.ds(pl.multiple_of(c * COLS, COLS), COLS)

    def down_copy(c, k):
        return pltpu.make_async_copy(
            down_hbm.at[0, pl.ds(k * depth, depth), cols(c)], dbuf.at[k], d_sem.at[k]
        )

    def qkv_copy(j):
        return pltpu.make_async_copy(
            qkv_hbm.at[0, pl.ds(pl.multiple_of(j * COLS, COLS), COLS), :], qbuf.at[j], q_sem.at[j]
        )

    hid_copy = pltpu.make_async_copy(hid_hbm.at[0], hid_v, small_sem.at[0])
    res_copy = pltpu.make_async_copy(res_hbm.at[0], res_v, small_sem.at[1])
    gain_copy = pltpu.make_async_copy(gain_hbm, gain_v, small_sem.at[2])
    hid_copy.start()
    for k in range(K_BLOCKS):
        down_copy(0, k).start()
    res_copy.start()
    gain_copy.start()

    barrier = pltpu.get_barrier_semaphore()
    for target in (
        (dp, pipe, other), (dp, after, core), (dp, after, other), (dp, before, core), (dp, before, other)
    ):
        pl.semaphore_signal(barrier, inc=1, device_id=target, device_id_type=MESH)

    def group_copy(c):
        return pltpu.make_async_remote_copy(
            src_ref=group.at[c, other_rows],
            dst_ref=group_in.at[c],
            send_sem=g_send.at[c],
            recv_sem=g_recv.at[c],
            device_id=(dp, pipe, other),
            device_id_type=MESH,
        )

    def x_copy(c, to):
        return pltpu.make_async_remote_copy(
            src_ref=stage.at[c],
            dst_ref=x_in.at[c, my_rows],
            send_sem=x_send.at[to, c],
            recv_sem=x_recv.at[core, c],
            device_id=(dp, after, to),
            device_id_type=MESH,
        )

    def x_arrival(c, source):
        rows = pl.ds(source * mine, mine)
        return pltpu.make_async_remote_copy(
            src_ref=stage.at[c],
            dst_ref=x_in.at[c, rows],
            send_sem=x_send.at[source, c],
            recv_sem=x_recv.at[source, c],
            device_id=(dp, after, core),
            device_id_type=MESH,
        )

    def finish(c):
        group_copy(c).wait_recv()
        total = group[c, my_rows, :].astype(jnp.float32) + group_in[c].astype(jnp.float32)
        rows = (res_v[:, cols(c)].astype(jnp.float32) + total).astype(jnp.bfloat16)
        stage[c] = rows
        out_v[:, cols(c)] = rows
        for to in range(2):
            x_copy(c, to).start()

    hid_copy.wait()

    def down_step(c, carry):
        total = None
        for k in range(K_BLOCKS):
            down_copy(c, k).wait()
            term = jnp.dot(
                hid_v[:, k * depth:(k + 1) * depth], dbuf[k], preferred_element_type=jnp.float32
            )
            total = term if total is None else total + term

            @pl.when(c < chunks - 1)
            def _():
                down_copy(c + 1, k).start()

            @pl.when(c == chunks - 1)
            def _():
                for j in range(k * chunks // K_BLOCKS, (k + 1) * chunks // K_BLOCKS):
                    qkv_copy(j).start()

        group[c] = total.astype(jnp.bfloat16)

        @pl.when(c == 0)
        def _():
            res_copy.wait()
            pl.semaphore_wait(barrier, 5)

        group_copy(c).start()

        @pl.when(c >= 1)
        def _():
            finish(c - 1)

        return carry

    lax.fori_loop(0, chunks, down_step, 0)
    gain_copy.wait()
    acc_v[...] = jnp.zeros_like(acc_v)
    sumsq[...] = jnp.zeros_like(sumsq)

    def qkv_step(j, carry):
        for source in range(2):
            x_arrival(j, source).wait_recv()
        x = x_in[j].astype(jnp.float32)
        squares = x * x
        part = squares[:, :128]
        for i in range(1, COLS // 128):
            part = part + squares[:, i * 128:(i + 1) * 128]
        sumsq[...] += part
        scaled = (x * gain_v[:, cols(j)]).astype(jnp.bfloat16)
        qkv_copy(j).wait()
        for n in range(q_parts):
            at = slice(n * COLS, (n + 1) * COLS)
            acc_v[:, at] += jnp.dot(scaled, qbuf[j, :, at], preferred_element_type=jnp.float32)

        @pl.when(j == 0)
        def _():
            finish(chunks - 1)
            pltpu.make_async_copy(out_v, out_hbm.at[0], small_sem.at[0]).start()

        return carry

    lax.fori_loop(0, chunks, qkv_step, 0)
    scaler = lax.rsqrt(jnp.sum(sumsq[...], axis=-1, keepdims=True) / width + EPS)

    def proj_copy(n):
        at = pl.ds(n * COLS, COLS)
        return pltpu.make_async_copy(proj_v.at[:, at], proj_hbm.at[0, :, at], o_sem.at[n])

    for n in range(q_parts):
        at = slice(n * COLS, (n + 1) * COLS)
        proj_v[:, at] = (acc_v[:, at] * scaler).astype(jnp.bfloat16)
        proj_copy(n).start()

    pltpu.make_async_copy(out_v, out_hbm.at[0], small_sem.at[0]).wait()

    def drain(c, carry):
        group_copy(c).wait_send()
        for to in range(2):
            x_copy(c, to).wait_send()
        return carry

    lax.fori_loop(0, chunks, drain, 0)
    for n in range(q_parts):
        proj_copy(n).wait()


def kernel_shards(pipes, hidden, residual, norm_gain, down_weight, qkv_weight):
    tokens, units = hidden.shape[1:]
    mine, width = residual.shape[1:]
    q_cols = qkv_weight.shape[2]
    chunks = width // COLS
    bf16 = jnp.bfloat16
    any_space = pl.BlockSpec(memory_space=pl.ANY)
    flops = 2 * tokens * width * (units + q_cols)
    return pl.pallas_call(
        functools.partial(boundary_kernel, pipes),
        out_shape=(
            jax.ShapeDtypeStruct((1, mine, width), bf16),
            jax.ShapeDtypeStruct((1, tokens, q_cols), bf16),
        ),
        in_specs=[any_space] * 5,
        out_specs=(any_space, any_space),
        scratch_shapes=[
            pltpu.VMEM((tokens, units), bf16),
            pltpu.VMEM((mine, width), bf16),
            pltpu.VMEM((1, width), jnp.float32),
            pltpu.VMEM((K_BLOCKS, units // K_BLOCKS, COLS), bf16),
            pltpu.VMEM((chunks, COLS, q_cols), bf16),
            pltpu.VMEM((chunks, tokens, COLS), bf16),
            pltpu.VMEM((chunks, mine, COLS), bf16),
            pltpu.VMEM((chunks, mine, COLS), bf16),
            pltpu.VMEM((chunks, tokens, COLS), bf16),
            pltpu.VMEM((mine, width), bf16),
            pltpu.VMEM((tokens, q_cols), bf16),
            pltpu.VMEM((tokens, q_cols), jnp.float32),
            pltpu.VMEM((tokens, 128), jnp.float32),
            pltpu.SemaphoreType.DMA((3,)),
            pltpu.SemaphoreType.DMA((K_BLOCKS,)),
            pltpu.SemaphoreType.DMA((chunks,)),
            pltpu.SemaphoreType.DMA((q_cols // COLS,)),
            pltpu.SemaphoreType.DMA((chunks,)),
            pltpu.SemaphoreType.DMA((chunks,)),
            pltpu.SemaphoreType.DMA((2, chunks)),
            pltpu.SemaphoreType.DMA((2, chunks)),
        ],
        compiler_params=pltpu.CompilerParams(
            collective_id=0, has_side_effects=True, vmem_limit_bytes=56 * 1024 * 1024
        ),
        cost_estimate=pl.CostEstimate(
            flops=flops, bytes_accessed=2 * width * (units + q_cols), transcendentals=0
        ),
    )(hidden, residual, norm_gain, down_weight, qkv_weight)


def solution(mesh):
    pipes = mesh.shape["pipe"]
    if mesh.shape["tensor"] == 2 and pipes > 2:
        shards = functools.partial(kernel_shards, pipes)
    else:
        shards = plain_shards
    return jax.shard_map(
        shards,
        mesh=mesh,
        in_specs=(
            P("pipe", "dp", "tensor"),
            P("pipe", ("dp", "tensor"), None),
            P("pipe", None),
            P("pipe", "tensor", None),
            P("pipe", None, "tensor"),
        ),
        out_specs=(P("pipe", ("dp", "tensor"), None), P("pipe", "dp", "tensor")),
        check_vma=False,
    )
```

```python
import functools

import jax
import jax.numpy as jnp
from jax import lax
from jax.experimental import pallas as pl
from jax.experimental.pallas import tpu as pltpu
from jax.sharding import PartitionSpec as P

EPS = 1e-05
COLS = 512
K_BLOCKS = 4
RING = 2
MESH = pl.DeviceIdType.MESH


def passed_along(value, axis, steps):
    count = lax.axis_size(axis)
    pairs = [(source, (source + steps) % count) for source in range(count)]
    return lax.ppermute(value, axis, pairs)


def normalize(values, gain_row):
    wide = values.astype(jnp.float32)
    scaler = lax.rsqrt(jnp.mean(wide * wide, axis=-1, keepdims=True) + EPS)
    return (wide * scaler * gain_row).astype(jnp.bfloat16)


def plain_shards(hidden, residual, norm_gain, down_weight, qkv_weight):
    hidden_rows = hidden[0]
    resid_rows = residual[0]
    gain_row = norm_gain[0]
    down_local = down_weight[0]
    qkv_local = qkv_weight[0]
    tok_rows = resid_rows.shape[0]
    resid_full = lax.all_gather(resid_rows, "tensor", axis=0, tiled=True)
    summed = lax.psum(
        jnp.dot(hidden_rows, down_local, preferred_element_type=jnp.float32).astype(jnp.bfloat16),
        "tensor",
    ).astype(jnp.float32)
    full_rows = (resid_full.astype(jnp.float32) + summed).astype(jnp.bfloat16)
    offset = lax.axis_index("tensor") * tok_rows
    section_output = lax.dynamic_slice_in_dim(full_rows, offset, tok_rows, 0)
    arrived = passed_along(full_rows, "pipe", 1)
    normed = normalize(arrived, gain_row)
    projections = jnp.dot(normed, qkv_local, preferred_element_type=jnp.float32).astype(
        jnp.bfloat16
    )
    return (section_output[None], projections[None])


def boundary_kernel(
    pipes,
    hid_hbm, res_hbm, gain_hbm, down_hbm, qkv_hbm,
    out_v, acc_v, sumsq,
    hid_v, res_v, gain_v, dbuf, qbuf, group, group_in, stage, x_in,
    small_sem, h_sem, d_sem, q_sem, g_send, g_recv, x_send, x_recv,
):
    dp = lax.axis_index("dp")
    pipe = lax.axis_index("pipe")
    core = lax.axis_index("tensor")
    other = 1 - core
    after = lax.rem(pipe + 1, pipes)
    before = lax.rem(pipe + pipes - 1, pipes)

    tokens, units = hid_v.shape
    mine, width = res_v.shape
    chunks = width // COLS
    depth = units // K_BLOCKS
    q_cols = qbuf.shape[2]
    q_parts = q_cols // COLS
    my_rows = pl.ds(pl.multiple_of(core * mine, mine), mine)
    other_rows = pl.ds(pl.multiple_of(other * mine, mine), mine)

    def cols(c):
        return pl.ds(pl.multiple_of(c * COLS, COLS), COLS)

    def down_copy(c, k):
        slot = lax.rem(c, RING) * K_BLOCKS + k
        return pltpu.make_async_copy(
            down_hbm.at[0, pl.ds(k * depth, depth), cols(c)], dbuf.at[slot], d_sem.at[slot]
        )

    def hid_copy(k):
        at = pl.ds(k * depth, depth)
        return pltpu.make_async_copy(hid_hbm.at[0, :, at], hid_v.at[:, at], h_sem.at[k])

    def qkv_copy(j):
        return pltpu.make_async_copy(
            qkv_hbm.at[0, pl.ds(pl.multiple_of(j * COLS, COLS), COLS), :], qbuf.at[j], q_sem.at[j]
        )

    res_copy = pltpu.make_async_copy(res_hbm.at[0], res_v, small_sem.at[0])
    gain_copy = pltpu.make_async_copy(gain_hbm, gain_v, small_sem.at[1])
    for k in range(K_BLOCKS):
        hid_copy(k).start()
        down_copy(jnp.int32(0), k).start()
    res_copy.start()
    gain_copy.start()
    for c in range(1, RING):
        for k in range(K_BLOCKS):
            down_copy(jnp.int32(c), k).start()

    barrier = pltpu.get_barrier_semaphore()
    for target in (
        (dp, pipe, other), (dp, after, core), (dp, after, other), (dp, before, core), (dp, before, other)
    ):
        pl.semaphore_signal(barrier, inc=1, device_id=target, device_id_type=MESH)

    def group_copy(c):
        return pltpu.make_async_remote_copy(
            src_ref=group.at[c, other_rows],
            dst_ref=group_in.at[c],
            send_sem=g_send.at[c],
            recv_sem=g_recv.at[c],
            device_id=(dp, pipe, other),
            device_id_type=MESH,
        )

    def x_copy(c, to):
        return pltpu.make_async_remote_copy(
            src_ref=stage.at[c],
            dst_ref=x_in.at[c, my_rows],
            send_sem=x_send.at[to, c],
            recv_sem=x_recv.at[core, c],
            device_id=(dp, after, to),
            device_id_type=MESH,
        )

    def x_arrival(c, source):
        rows = pl.ds(source * mine, mine)
        return pltpu.make_async_remote_copy(
            src_ref=stage.at[c],
            dst_ref=x_in.at[c, rows],
            send_sem=x_send.at[source, c],
            recv_sem=x_recv.at[source, c],
            device_id=(dp, after, core),
            device_id_type=MESH,
        )

    def finish(c):
        group_copy(c).wait_recv()
        total = group[c, my_rows, :].astype(jnp.float32) + group_in[c].astype(jnp.float32)
        rows = (res_v[:, cols(c)].astype(jnp.float32) + total).astype(jnp.bfloat16)
        stage[c] = rows
        out_v[:, cols(c)] = rows
        for to in range(2):
            x_copy(c, to).start()

    def down_step(c, carry):
        total = None
        for k in range(K_BLOCKS):

            @pl.when(c == 0)
            def _():
                hid_copy(k).wait()

            down_copy(c, k).wait()
            term = jnp.dot(
                hid_v[:, k * depth:(k + 1) * depth],
                dbuf[lax.rem(c, RING) * K_BLOCKS + k],
                preferred_element_type=jnp.float32,
            )
            total = term if total is None else total + term

            @pl.when(c < chunks - RING)
            def _():
                down_copy(c + RING, k).start()

            @pl.when(c >= chunks - RING)
            def _():
                qkv_copy((c - (chunks - RING)) * K_BLOCKS + k).start()

        group[c] = total.astype(jnp.bfloat16)

        @pl.when(c == 0)
        def _():
            res_copy.wait()
            pl.semaphore_wait(barrier, 5)

        group_copy(c).start()

        @pl.when(c >= 1)
        def _():
            finish(c - 1)

        return carry

    lax.fori_loop(0, chunks, down_step, 0)
    gain_copy.wait()
    acc_v[...] = jnp.zeros_like(acc_v)
    sumsq[...] = jnp.zeros_like(sumsq)

    def qkv_step(j, carry):
        for source in range(2):
            x_arrival(j, source).wait_recv()
        x = x_in[j].astype(jnp.float32)
        squares = x * x
        part = squares[:, :128]
        for i in range(1, COLS // 128):
            part = part + squares[:, i * 128:(i + 1) * 128]
        sumsq[...] += part
        scaled = (x * gain_v[:, cols(j)]).astype(jnp.bfloat16)
        qkv_copy(j).wait()
        for n in range(q_parts):
            at = slice(n * COLS, (n + 1) * COLS)
            acc_v[:, at] += jnp.dot(scaled, qbuf[j, :, at], preferred_element_type=jnp.float32)

        @pl.when(j == 0)
        def _():
            finish(chunks - 1)

        return carry

    lax.fori_loop(0, chunks, qkv_step, 0)

    def drain(c, carry):
        group_copy(c).wait_send()
        for to in range(2):
            x_copy(c, to).wait_send()
        return carry

    lax.fori_loop(0, chunks, drain, 0)


def write_kernel(rows_v, acc_v, sumsq, out_hbm, proj_hbm, proj_v, r_sem, o_sem):
    width = rows_v.shape[1]
    q_cols = acc_v.shape[1]
    rows_copy = pltpu.make_async_copy(rows_v, out_hbm.at[0], r_sem)
    rows_copy.start()
    scaler = lax.rsqrt(jnp.sum(sumsq[...], axis=-1, keepdims=True) / width + EPS)
    copies = []
    for n in range(q_cols // COLS):
        at = slice(n * COLS, (n + 1) * COLS)
        proj_v[:, at] = (acc_v[:, at] * scaler).astype(jnp.bfloat16)
        copy = pltpu.make_async_copy(proj_v.at[:, at], proj_hbm.at[0, :, at], o_sem.at[n])
        copy.start()
        copies.append(copy)
    for copy in [rows_copy] + copies:
        copy.wait()


def kernel_shards(pipes, hidden, residual, norm_gain, down_weight, qkv_weight):
    tokens, units = hidden.shape[1:]
    mine, width = residual.shape[1:]
    q_cols = qkv_weight.shape[2]
    chunks = width // COLS
    bf16 = jnp.bfloat16
    any_space = pl.BlockSpec(memory_space=pl.ANY)
    flops = 2 * tokens * width * (units + q_cols)
    vmem_space = pl.BlockSpec(memory_space=pltpu.VMEM)
    rows, acc, sumsq = pl.pallas_call(
        functools.partial(boundary_kernel, pipes),
        out_shape=(
            pltpu.VMEM((mine, width), bf16),
            pltpu.VMEM((tokens, q_cols), jnp.float32),
            pltpu.VMEM((tokens, 128), jnp.float32),
        ),
        in_specs=[any_space] * 5,
        out_specs=(vmem_space,) * 3,
        scratch_shapes=[
            pltpu.VMEM((tokens, units), bf16),
            pltpu.VMEM((mine, width), bf16),
            pltpu.VMEM((1, width), jnp.float32),
            pltpu.VMEM((RING * K_BLOCKS, units // K_BLOCKS, COLS), bf16),
            pltpu.VMEM((chunks, COLS, q_cols), bf16),
            pltpu.VMEM((chunks, tokens, COLS), bf16),
            pltpu.VMEM((chunks, mine, COLS), bf16),
            pltpu.VMEM((chunks, mine, COLS), bf16),
            pltpu.VMEM((chunks, tokens, COLS), bf16),
            pltpu.SemaphoreType.DMA((2,)),
            pltpu.SemaphoreType.DMA((K_BLOCKS,)),
            pltpu.SemaphoreType.DMA((RING * K_BLOCKS,)),
            pltpu.SemaphoreType.DMA((chunks,)),
            pltpu.SemaphoreType.DMA((chunks,)),
            pltpu.SemaphoreType.DMA((chunks,)),
            pltpu.SemaphoreType.DMA((2, chunks)),
            pltpu.SemaphoreType.DMA((2, chunks)),
        ],
        compiler_params=pltpu.CompilerParams(
            collective_id=0, has_side_effects=True, vmem_limit_bytes=56 * 1024 * 1024
        ),
        cost_estimate=pl.CostEstimate(
            flops=flops, bytes_accessed=2 * width * (units + q_cols), transcendentals=0
        ),
    )(hidden, residual, norm_gain, down_weight, qkv_weight)
    return pl.pallas_call(
        write_kernel,
        out_shape=(
            jax.ShapeDtypeStruct((1, mine, width), bf16),
            jax.ShapeDtypeStruct((1, tokens, q_cols), bf16),
        ),
        in_specs=[vmem_space] * 3,
        out_specs=(any_space, any_space),
        scratch_shapes=[
            pltpu.VMEM((tokens, q_cols), bf16),
            pltpu.SemaphoreType.DMA,
            pltpu.SemaphoreType.DMA((q_cols // COLS,)),
        ],
    )(rows, acc, sumsq)


def solution(mesh):
    pipes = mesh.shape["pipe"]
    if mesh.shape["tensor"] == 2 and pipes > 2:
        shards = functools.partial(kernel_shards, pipes)
    else:
        shards = plain_shards
    return jax.shard_map(
        shards,
        mesh=mesh,
        in_specs=(
            P("pipe", "dp", "tensor"),
            P("pipe", ("dp", "tensor"), None),
            P("pipe", None),
            P("pipe", "tensor", None),
            P("pipe", None, "tensor"),
        ),
        out_specs=(P("pipe", ("dp", "tensor"), None), P("pipe", "dp", "tensor")),
        check_vma=False,
    )
```

```python
import functools

import jax
import jax.numpy as jnp
from jax import lax
from jax.experimental import pallas as pl
from jax.experimental.pallas import tpu as pltpu
from jax.sharding import PartitionSpec as P

EPS = 1e-05
COLS = 512
K_BLOCKS = 4
RING = 2
MESH = pl.DeviceIdType.MESH


def passed_along(value, axis, steps):
    count = lax.axis_size(axis)
    pairs = [(source, (source + steps) % count) for source in range(count)]
    return lax.ppermute(value, axis, pairs)


def normalize(values, gain_row):
    wide = values.astype(jnp.float32)
    scaler = lax.rsqrt(jnp.mean(wide * wide, axis=-1, keepdims=True) + EPS)
    return (wide * scaler * gain_row).astype(jnp.bfloat16)


def plain_shards(hidden, residual, norm_gain, down_weight, qkv_weight):
    hidden_rows = hidden[0]
    resid_rows = residual[0]
    gain_row = norm_gain[0]
    down_local = down_weight[0]
    qkv_local = qkv_weight[0]
    tok_rows = resid_rows.shape[0]
    resid_full = lax.all_gather(resid_rows, "tensor", axis=0, tiled=True)
    summed = lax.psum(
        jnp.dot(hidden_rows, down_local, preferred_element_type=jnp.float32).astype(jnp.bfloat16),
        "tensor",
    ).astype(jnp.float32)
    full_rows = (resid_full.astype(jnp.float32) + summed).astype(jnp.bfloat16)
    offset = lax.axis_index("tensor") * tok_rows
    section_output = lax.dynamic_slice_in_dim(full_rows, offset, tok_rows, 0)
    arrived = passed_along(full_rows, "pipe", 1)
    normed = normalize(arrived, gain_row)
    projections = jnp.dot(normed, qkv_local, preferred_element_type=jnp.float32).astype(
        jnp.bfloat16
    )
    return (section_output[None], projections[None])


def boundary_kernel(
    pipes,
    hid_hbm, res_hbm, gain_hbm, down_hbm, qkv_hbm,
    out_v, acc_v, sumsq,
    hid_v, res_v, gain_v, dbuf, qbuf, group, group_in, stage, x_in,
    small_sem, h_sem, d_sem, q_sem, g_send, g_recv, x_send, x_recv,
):
    dp = lax.axis_index("dp")
    pipe = lax.axis_index("pipe")
    core = lax.axis_index("tensor")
    other = 1 - core
    after = lax.rem(pipe + 1, pipes)
    before = lax.rem(pipe + pipes - 1, pipes)

    tokens, units = hid_v.shape
    mine, width = res_v.shape
    chunks = width // COLS
    depth = units // K_BLOCKS
    q_cols = qbuf.shape[2]
    q_parts = q_cols // COLS
    q_half = q_cols // 2
    my_rows = pl.ds(pl.multiple_of(core * mine, mine), mine)
    other_rows = pl.ds(pl.multiple_of(other * mine, mine), mine)

    def cols(c):
        return pl.ds(pl.multiple_of(c * COLS, COLS), COLS)

    def down_copy(c, k):
        slot = lax.rem(c, RING) * K_BLOCKS + k
        return pltpu.make_async_copy(
            down_hbm.at[0, pl.ds(k * depth, depth), cols(c)], dbuf.at[slot], d_sem.at[slot]
        )

    def hid_copy(k):
        at = pl.ds(k * depth, depth)
        return pltpu.make_async_copy(hid_hbm.at[0, :, at], hid_v.at[:, at], h_sem.at[k])

    def qkv_copy(j, half):
        at = pl.ds(half * q_half, q_half)
        return pltpu.make_async_copy(
            qkv_hbm.at[0, cols(j), at], qbuf.at[j, :, at], q_sem.at[half, j]
        )

    res_copy = pltpu.make_async_copy(res_hbm.at[0], res_v, small_sem.at[0])
    gain_copy = pltpu.make_async_copy(gain_hbm, gain_v, small_sem.at[1])
    for k in range(K_BLOCKS):
        hid_copy(k).start()
        down_copy(jnp.int32(0), k).start()
    res_copy.start()
    gain_copy.start()
    for c in range(1, RING):
        for k in range(K_BLOCKS):
            down_copy(jnp.int32(c), k).start()

    barrier = pltpu.get_barrier_semaphore()
    for target in (
        (dp, pipe, other), (dp, after, core), (dp, after, other), (dp, before, core), (dp, before, other)
    ):
        pl.semaphore_signal(barrier, inc=1, device_id=target, device_id_type=MESH)

    def group_copy(c):
        return pltpu.make_async_remote_copy(
            src_ref=group.at[c, other_rows],
            dst_ref=group_in.at[c],
            send_sem=g_send.at[c],
            recv_sem=g_recv.at[c],
            device_id=(dp, pipe, other),
            device_id_type=MESH,
        )

    def x_copy(c, to):
        return pltpu.make_async_remote_copy(
            src_ref=stage.at[c],
            dst_ref=x_in.at[c, my_rows],
            send_sem=x_send.at[to, c],
            recv_sem=x_recv.at[core, c],
            device_id=(dp, after, to),
            device_id_type=MESH,
        )

    def x_arrival(c, source):
        rows = pl.ds(source * mine, mine)
        return pltpu.make_async_remote_copy(
            src_ref=stage.at[c],
            dst_ref=x_in.at[c, rows],
            send_sem=x_send.at[source, c],
            recv_sem=x_recv.at[source, c],
            device_id=(dp, after, core),
            device_id_type=MESH,
        )

    def finish(c):
        group_copy(c).wait_recv()
        total = group[c, my_rows, :].astype(jnp.float32) + group_in[c].astype(jnp.float32)
        rows = (res_v[:, cols(c)].astype(jnp.float32) + total).astype(jnp.bfloat16)
        stage[c] = rows
        out_v[:, cols(c)] = rows
        for to in range(2):
            x_copy(c, to).start()

    def down_step(c, carry):
        total = None
        for k in range(K_BLOCKS):

            @pl.when(c == 0)
            def _():
                hid_copy(k).wait()

            down_copy(c, k).wait()
            term = jnp.dot(
                hid_v[:, k * depth:(k + 1) * depth],
                dbuf[lax.rem(c, RING) * K_BLOCKS + k],
                preferred_element_type=jnp.float32,
            )
            total = term if total is None else total + term

            @pl.when(c < chunks - RING)
            def _():
                down_copy(c + RING, k).start()

            @pl.when(c >= chunks - RING)
            def _():
                for half in range(2):
                    qkv_copy((c - (chunks - RING)) * K_BLOCKS + k, half).start()

        group[c] = total.astype(jnp.bfloat16)

        @pl.when(c == 0)
        def _():
            res_copy.wait()
            pl.semaphore_wait(barrier, 5)

        group_copy(c).start()

        @pl.when(c >= 1)
        def _():
            finish(c - 1)

        return carry

    lax.fori_loop(0, chunks, down_step, 0)
    gain_copy.wait()
    acc_v[...] = jnp.zeros_like(acc_v)
    sumsq[...] = jnp.zeros_like(sumsq)

    def qkv_step(j, carry):
        for source in range(2):
            x_arrival(j, source).wait_recv()
        x = x_in[j].astype(jnp.float32)
        squares = x * x
        part = squares[:, :128]
        for i in range(1, COLS // 128):
            part = part + squares[:, i * 128:(i + 1) * 128]
        sumsq[...] += part
        scaled = (x * gain_v[:, cols(j)]).astype(jnp.bfloat16)
        for n in range(q_parts):
            if n * COLS % q_half == 0:
                qkv_copy(j, n * COLS // q_half).wait()
            at = slice(n * COLS, (n + 1) * COLS)
            acc_v[:, at] += jnp.dot(scaled, qbuf[j, :, at], preferred_element_type=jnp.float32)

        @pl.when(j == 0)
        def _():
            finish(chunks - 1)

        return carry

    lax.fori_loop(0, chunks, qkv_step, 0)

    def drain(c, carry):
        group_copy(c).wait_send()
        for to in range(2):
            x_copy(c, to).wait_send()
        return carry

    lax.fori_loop(0, chunks, drain, 0)


def write_kernel(rows_v, acc_v, sumsq, out_hbm, proj_hbm, proj_v, r_sem, o_sem):
    width = rows_v.shape[1]
    q_cols = acc_v.shape[1]
    rows_copy = pltpu.make_async_copy(rows_v, out_hbm.at[0], r_sem)
    rows_copy.start()
    scaler = lax.rsqrt(jnp.sum(sumsq[...], axis=-1, keepdims=True) / width + EPS)
    copies = []
    for n in range(q_cols // COLS):
        at = slice(n * COLS, (n + 1) * COLS)
        proj_v[:, at] = (acc_v[:, at] * scaler).astype(jnp.bfloat16)
        copy = pltpu.make_async_copy(proj_v.at[:, at], proj_hbm.at[0, :, at], o_sem.at[n])
        copy.start()
        copies.append(copy)
    for copy in [rows_copy] + copies:
        copy.wait()


def kernel_shards(pipes, hidden, residual, norm_gain, down_weight, qkv_weight):
    tokens, units = hidden.shape[1:]
    mine, width = residual.shape[1:]
    q_cols = qkv_weight.shape[2]
    chunks = width // COLS
    bf16 = jnp.bfloat16
    any_space = pl.BlockSpec(memory_space=pl.ANY)
    flops = 2 * tokens * width * (units + q_cols)
    vmem_space = pl.BlockSpec(memory_space=pltpu.VMEM)
    rows, acc, sumsq = pl.pallas_call(
        functools.partial(boundary_kernel, pipes),
        out_shape=(
            pltpu.VMEM((mine, width), bf16),
            pltpu.VMEM((tokens, q_cols), jnp.float32),
            pltpu.VMEM((tokens, 128), jnp.float32),
        ),
        in_specs=[any_space] * 5,
        out_specs=(vmem_space,) * 3,
        scratch_shapes=[
            pltpu.VMEM((tokens, units), bf16),
            pltpu.VMEM((mine, width), bf16),
            pltpu.VMEM((1, width), jnp.float32),
            pltpu.VMEM((RING * K_BLOCKS, units // K_BLOCKS, COLS), bf16),
            pltpu.VMEM((chunks, COLS, q_cols), bf16),
            pltpu.VMEM((chunks, tokens, COLS), bf16),
            pltpu.VMEM((chunks, mine, COLS), bf16),
            pltpu.VMEM((chunks, mine, COLS), bf16),
            pltpu.VMEM((chunks, tokens, COLS), bf16),
            pltpu.SemaphoreType.DMA((2,)),
            pltpu.SemaphoreType.DMA((K_BLOCKS,)),
            pltpu.SemaphoreType.DMA((RING * K_BLOCKS,)),
            pltpu.SemaphoreType.DMA((2, chunks)),
            pltpu.SemaphoreType.DMA((chunks,)),
            pltpu.SemaphoreType.DMA((chunks,)),
            pltpu.SemaphoreType.DMA((2, chunks)),
            pltpu.SemaphoreType.DMA((2, chunks)),
        ],
        compiler_params=pltpu.CompilerParams(
            collective_id=0, has_side_effects=True, vmem_limit_bytes=56 * 1024 * 1024
        ),
        cost_estimate=pl.CostEstimate(
            flops=flops, bytes_accessed=2 * width * (units + q_cols), transcendentals=0
        ),
    )(hidden, residual, norm_gain, down_weight, qkv_weight)
    return pl.pallas_call(
        write_kernel,
        out_shape=(
            jax.ShapeDtypeStruct((1, mine, width), bf16),
            jax.ShapeDtypeStruct((1, tokens, q_cols), bf16),
        ),
        in_specs=[vmem_space] * 3,
        out_specs=(any_space, any_space),
        scratch_shapes=[
            pltpu.VMEM((tokens, q_cols), bf16),
            pltpu.SemaphoreType.DMA,
            pltpu.SemaphoreType.DMA((q_cols // COLS,)),
        ],
        compiler_params=pltpu.CompilerParams(vmem_limit_bytes=8 * 1024 * 1024),
    )(*(pltpu.with_memory_space_constraint(held, pltpu.VMEM) for held in (rows, acc, sumsq)))


def solution(mesh):
    pipes = mesh.shape["pipe"]
    if mesh.shape["tensor"] == 2 and pipes > 2:
        shards = functools.partial(kernel_shards, pipes)
    else:
        shards = plain_shards
    return jax.shard_map(
        shards,
        mesh=mesh,
        in_specs=(
            P("pipe", "dp", "tensor"),
            P("pipe", ("dp", "tensor"), None),
            P("pipe", None),
            P("pipe", "tensor", None),
            P("pipe", None, "tensor"),
        ),
        out_specs=(P("pipe", ("dp", "tensor"), None), P("pipe", "dp", "tensor")),
        check_vma=False,
    )
```

```python
import functools

import jax
import jax.numpy as jnp
from jax import lax
from jax.experimental import pallas as pl
from jax.experimental.pallas import tpu as pltpu
from jax.sharding import PartitionSpec as P

EPS = 1e-05
COLS = 512
K_BLOCKS = 4
RING = 2
MESH = pl.DeviceIdType.MESH


def passed_along(value, axis, steps):
    count = lax.axis_size(axis)
    pairs = [(source, (source + steps) % count) for source in range(count)]
    return lax.ppermute(value, axis, pairs)


def normalize(values, gain_row):
    wide = values.astype(jnp.float32)
    scaler = lax.rsqrt(jnp.mean(wide * wide, axis=-1, keepdims=True) + EPS)
    return (wide * scaler * gain_row).astype(jnp.bfloat16)


def plain_shards(hidden, residual, norm_gain, down_weight, qkv_weight):
    hidden_rows = hidden[0]
    resid_rows = residual[0]
    gain_row = norm_gain[0]
    down_local = down_weight[0]
    qkv_local = qkv_weight[0]
    tok_rows = resid_rows.shape[0]
    resid_full = lax.all_gather(resid_rows, "tensor", axis=0, tiled=True)
    summed = lax.psum(
        jnp.dot(hidden_rows, down_local, preferred_element_type=jnp.float32).astype(jnp.bfloat16),
        "tensor",
    ).astype(jnp.float32)
    full_rows = (resid_full.astype(jnp.float32) + summed).astype(jnp.bfloat16)
    offset = lax.axis_index("tensor") * tok_rows
    section_output = lax.dynamic_slice_in_dim(full_rows, offset, tok_rows, 0)
    arrived = passed_along(full_rows, "pipe", 1)
    normed = normalize(arrived, gain_row)
    projections = jnp.dot(normed, qkv_local, preferred_element_type=jnp.float32).astype(
        jnp.bfloat16
    )
    return (section_output[None], projections[None])


def boundary_kernel(
    pipes,
    hid_hbm, res_hbm, gain_hbm, down_hbm, qkv_hbm,
    out_v, acc_v, sumsq,
    hid_v, res_v, gain_v, dbuf, qbuf, group, group_in, stage, x_in,
    small_sem, h_sem, d_sem, q_sem, g_send, g_recv, x_send, x_recv,
):
    dp = lax.axis_index("dp")
    pipe = lax.axis_index("pipe")
    core = lax.axis_index("tensor")
    other = 1 - core
    after = lax.rem(pipe + 1, pipes)
    before = lax.rem(pipe + pipes - 1, pipes)

    tokens, units = hid_v.shape
    mine, width = res_v.shape
    chunks = width // COLS
    depth = units // K_BLOCKS
    q_cols = qbuf.shape[2]
    q_parts = q_cols // COLS
    q_half = q_cols // 2
    my_rows = pl.ds(pl.multiple_of(core * mine, mine), mine)
    other_rows = pl.ds(pl.multiple_of(other * mine, mine), mine)

    def cols(c):
        return pl.ds(pl.multiple_of(c * COLS, COLS), COLS)

    def down_copy(c, k):
        slot = lax.rem(c, RING) * K_BLOCKS + k
        return pltpu.make_async_copy(
            down_hbm.at[0, pl.ds(k * depth, depth), cols(c)], dbuf.at[slot], d_sem.at[slot]
        )

    def hid_copy(k):
        at = pl.ds(k * depth, depth)
        return pltpu.make_async_copy(hid_hbm.at[0, :, at], hid_v.at[:, at], h_sem.at[k])

    def qkv_copy(j, half):
        at = pl.ds(half * q_half, q_half)
        return pltpu.make_async_copy(
            qkv_hbm.at[0, cols(j), at], qbuf.at[j, :, at], q_sem.at[half, j]
        )

    res_copy = pltpu.make_async_copy(res_hbm.at[0], res_v, small_sem.at[0])
    gain_copy = pltpu.make_async_copy(gain_hbm, gain_v, small_sem.at[1])
    for k in range(K_BLOCKS):
        hid_copy(k).start()
        down_copy(jnp.int32(0), k).start()
    res_copy.start()
    gain_copy.start()
    for c in range(1, RING):
        for k in range(K_BLOCKS):
            down_copy(jnp.int32(c), k).start()

    barrier = pltpu.get_barrier_semaphore()
    for target in (
        (dp, pipe, other), (dp, after, core), (dp, after, other), (dp, before, core), (dp, before, other)
    ):
        pl.semaphore_signal(barrier, inc=1, device_id=target, device_id_type=MESH)

    def group_copy(c):
        return pltpu.make_async_remote_copy(
            src_ref=group.at[c, other_rows],
            dst_ref=group_in.at[c],
            send_sem=g_send.at[c],
            recv_sem=g_recv.at[c],
            device_id=(dp, pipe, other),
            device_id_type=MESH,
        )

    def x_copy(c, to):
        return pltpu.make_async_remote_copy(
            src_ref=stage.at[c],
            dst_ref=x_in.at[c, my_rows],
            send_sem=x_send.at[to, c],
            recv_sem=x_recv.at[core, c],
            device_id=(dp, after, to),
            device_id_type=MESH,
        )

    def x_arrival(c, source):
        rows = pl.ds(source * mine, mine)
        return pltpu.make_async_remote_copy(
            src_ref=stage.at[c],
            dst_ref=x_in.at[c, rows],
            send_sem=x_send.at[source, c],
            recv_sem=x_recv.at[source, c],
            device_id=(dp, after, core),
            device_id_type=MESH,
        )

    def finish(c):
        group_copy(c).wait_recv()
        total = group[c, my_rows, :].astype(jnp.float32) + group_in[c].astype(jnp.float32)
        rows = (res_v[:, cols(c)].astype(jnp.float32) + total).astype(jnp.bfloat16)
        stage[c] = rows
        out_v[:, cols(c)] = rows
        for to in range(2):
            x_copy(c, to).start()

    def down_step(c, carry):
        total = None
        for k in range(K_BLOCKS):

            @pl.when(c == 0)
            def _():
                hid_copy(k).wait()

            down_copy(c, k).wait()
            term = jnp.dot(
                hid_v[:, k * depth:(k + 1) * depth],
                dbuf[lax.rem(c, RING) * K_BLOCKS + k],
                preferred_element_type=jnp.float32,
            )
            total = term if total is None else total + term

            @pl.when(c < chunks - RING)
            def _():
                down_copy(c + RING, k).start()

            @pl.when(c >= chunks - RING)
            def _():
                for half in range(2):
                    qkv_copy((c - (chunks - RING)) * K_BLOCKS + k, half).start()

        group[c] = total.astype(jnp.bfloat16)

        @pl.when(c == 0)
        def _():
            res_copy.wait()
            pl.semaphore_wait(barrier, 5)

        group_copy(c).start()

        @pl.when(c >= 1)
        def _():
            finish(c - 1)

        return carry

    lax.fori_loop(0, chunks, down_step, 0)
    finish(chunks - 1)
    gain_copy.wait()
    acc_v[...] = jnp.zeros_like(acc_v)
    sumsq[...] = jnp.zeros_like(sumsq)

    def qkv_step(j, carry):
        for source in range(2):
            x_arrival(j, source).wait_recv()
        x = x_in[j].astype(jnp.float32)
        squares = x * x
        part = squares[:, :128]
        for i in range(1, COLS // 128):
            part = part + squares[:, i * 128:(i + 1) * 128]
        sumsq[...] += part
        scaled = (x * gain_v[:, cols(j)]).astype(jnp.bfloat16)
        for n in range(q_parts):
            if n * COLS % q_half == 0:
                qkv_copy(j, n * COLS // q_half).wait()
            at = slice(n * COLS, (n + 1) * COLS)
            acc_v[:, at] += jnp.dot(scaled, qbuf[j, :, at], preferred_element_type=jnp.float32)

        return carry

    lax.fori_loop(0, chunks, qkv_step, 0)

    def drain(c, carry):
        group_copy(c).wait_send()
        for to in range(2):
            x_copy(c, to).wait_send()
        return carry

    lax.fori_loop(0, chunks, drain, 0)


def write_kernel(rows_v, acc_v, sumsq, out_hbm, proj_hbm, proj_v, r_sem, o_sem):
    width = rows_v.shape[1]
    q_cols = acc_v.shape[1]
    rows_copy = pltpu.make_async_copy(rows_v, out_hbm.at[0], r_sem)
    rows_copy.start()
    scaler = lax.rsqrt(jnp.sum(sumsq[...], axis=-1, keepdims=True) / width + EPS)
    copies = []
    for n in range(q_cols // COLS):
        at = slice(n * COLS, (n + 1) * COLS)
        proj_v[:, at] = (acc_v[:, at] * scaler).astype(jnp.bfloat16)
        copy = pltpu.make_async_copy(proj_v.at[:, at], proj_hbm.at[0, :, at], o_sem.at[n])
        copy.start()
        copies.append(copy)
    for copy in [rows_copy] + copies:
        copy.wait()


def kernel_shards(pipes, hidden, residual, norm_gain, down_weight, qkv_weight):
    tokens, units = hidden.shape[1:]
    mine, width = residual.shape[1:]
    q_cols = qkv_weight.shape[2]
    chunks = width // COLS
    bf16 = jnp.bfloat16
    any_space = pl.BlockSpec(memory_space=pl.ANY)
    flops = 2 * tokens * width * (units + q_cols)
    vmem_space = pl.BlockSpec(memory_space=pltpu.VMEM)
    rows, acc, sumsq = pl.pallas_call(
        functools.partial(boundary_kernel, pipes),
        out_shape=(
            pltpu.VMEM((mine, width), bf16),
            pltpu.VMEM((tokens, q_cols), jnp.float32),
            pltpu.VMEM((tokens, 128), jnp.float32),
        ),
        in_specs=[any_space] * 5,
        out_specs=(vmem_space,) * 3,
        scratch_shapes=[
            pltpu.VMEM((tokens, units), bf16),
            pltpu.VMEM((mine, width), bf16),
            pltpu.VMEM((1, width), jnp.float32),
            pltpu.VMEM((RING * K_BLOCKS, units // K_BLOCKS, COLS), bf16),
            pltpu.VMEM((chunks, COLS, q_cols), bf16),
            pltpu.VMEM((chunks, tokens, COLS), bf16),
            pltpu.VMEM((chunks, mine, COLS), bf16),
            pltpu.VMEM((chunks, mine, COLS), bf16),
            pltpu.VMEM((chunks, tokens, COLS), bf16),
            pltpu.SemaphoreType.DMA((2,)),
            pltpu.SemaphoreType.DMA((K_BLOCKS,)),
            pltpu.SemaphoreType.DMA((RING * K_BLOCKS,)),
            pltpu.SemaphoreType.DMA((2, chunks)),
            pltpu.SemaphoreType.DMA((chunks,)),
            pltpu.SemaphoreType.DMA((chunks,)),
            pltpu.SemaphoreType.DMA((2, chunks)),
            pltpu.SemaphoreType.DMA((2, chunks)),
        ],
        compiler_params=pltpu.CompilerParams(
            collective_id=0, has_side_effects=True, vmem_limit_bytes=56 * 1024 * 1024
        ),
        cost_estimate=pl.CostEstimate(
            flops=flops, bytes_accessed=2 * width * (units + q_cols), transcendentals=0
        ),
    )(hidden, residual, norm_gain, down_weight, qkv_weight)
    return pl.pallas_call(
        write_kernel,
        out_shape=(
            jax.ShapeDtypeStruct((1, mine, width), bf16),
            jax.ShapeDtypeStruct((1, tokens, q_cols), bf16),
        ),
        in_specs=[vmem_space] * 3,
        out_specs=(any_space, any_space),
        scratch_shapes=[
            pltpu.VMEM((tokens, q_cols), bf16),
            pltpu.SemaphoreType.DMA,
            pltpu.SemaphoreType.DMA((q_cols // COLS,)),
        ],
        compiler_params=pltpu.CompilerParams(vmem_limit_bytes=8 * 1024 * 1024),
    )(*(pltpu.with_memory_space_constraint(held, pltpu.VMEM) for held in (rows, acc, sumsq)))


def solution(mesh):
    pipes = mesh.shape["pipe"]
    if mesh.shape["tensor"] == 2 and pipes > 2:
        shards = functools.partial(kernel_shards, pipes)
    else:
        shards = plain_shards
    return jax.shard_map(
        shards,
        mesh=mesh,
        in_specs=(
            P("pipe", "dp", "tensor"),
            P("pipe", ("dp", "tensor"), None),
            P("pipe", None),
            P("pipe", "tensor", None),
            P("pipe", None, "tensor"),
        ),
        out_specs=(P("pipe", ("dp", "tensor"), None), P("pipe", "dp", "tensor")),
        check_vma=False,
    )
```
